32 devices in a mesh: row: 4 (over y, core), col: 8 (over z, x).
Axes of the slice: x: 2, y: 2, z: 4, core: 2. Of those that a mesh axis runs over, the one named last changes fastest.
Arguments:
- b_three: bfloat16 [64, 384, 1536], P(('row', 'col')), may hold values from -0.47851562 to 0.47851562
- e_occ: float32 [64], replicated, may hold values from -1.5 to -0.3
- e_vir: float32 [384], replicated, may hold values from 0.2 to 3
- c_occ: bfloat16 [768, 64], replicated, may hold values from -0.75 to 0.75
- pair_list: int32 [32, 8, 2], P(('row', 'col')), may hold values from 0 to 63, as said below
- pair_live: int32 [32, 8], P(('row', 'col')), may hold values from 0 to 1, as said below
Outputs:
- gamma_ao: bfloat16 [384, 1536, 768], P('row', 'col')
The draws below stay inside these ranges and needn't reach their ends.
Inputs may be any that keep to these rules, and one draw needn't show every extreme that they name: pair_list[w, p, 0] is one of the orbitals 2 w to 2 w + 1; pair_list[w, p, 1] is one of the orbitals 2 q to 2 q + 1 with q = (w // 8) * 8 + p. `pair_live`: every worker lists between 1 and 8 pairs; some worker lists all 8.
All inputs are finite; a program needn't handle non-finite values.
Results may differ from the reference program's by a relative error of at most 0.0053.
Values may be sent and summed in bfloat16 or wider, within the bound.
A program may use at most 128 MiB of HBM per device.

```python
import jax
import jax.numpy as jnp
from jax import lax

V = 384
X = 1536
NBF = 768
ORB_DEV = 2
WORKERS = 32
PEERS = 8
O = 64


def draw_pair_list(key, part):
    worker_ids = jnp.arange(WORKERS, dtype=jnp.int32)[:, None]
    peer_ids = jnp.arange(PEERS, dtype=jnp.int32)[None, :]
    first_pick = jax.random.randint(jax.random.fold_in(key, 11), (WORKERS, PEERS), 0, ORB_DEV)
    second_pick = jax.random.randint(jax.random.fold_in(key, 12), (WORKERS, PEERS), 0, ORB_DEV)
    first = ORB_DEV * worker_ids + first_pick
    owner = worker_ids // PEERS * PEERS + peer_ids
    second = ORB_DEV * owner + second_pick
    return jnp.stack([first, second], -1).astype(jnp.int32)


def draw_pair_live(key, part):
    counts = jax.random.randint(jax.random.fold_in(key, 21), (WORKERS,), 1, PEERS + 1)
    busiest = jax.random.randint(jax.random.fold_in(key, 22), (), 0, WORKERS)
    counts = jnp.where(jnp.arange(WORKERS) == busiest, PEERS, counts)
    subkeys = jax.random.split(jax.random.fold_in(key, 23), WORKERS)
    ranks = jax.vmap(lambda subkey: jax.random.permutation(subkey, PEERS))(subkeys)
    return (ranks < counts[:, None]).astype(jnp.int32)


def block_levels(own_key, shape, shards, low, top_value):
    def one(dim, blocks):
        draws = jax.random.uniform(jax.random.fold_in(jax.random.fold_in(own_key, 6), dim), (blocks,), jnp.float32, low / len(shards), top_value / len(shards))
        return jnp.repeat(jnp.exp(draws), shape[dim] // blocks).reshape((-1,) + (1,) * (len(shape) - dim - 1))

    gain = one(*shards[0])
    for cut in shards[1:]:
        gain = gain * one(*cut)
    return gain


def noise(key, extent, width, reach, cuts=(), held_as=jnp.bfloat16):
    gain = block_levels(key, extent, cuts, -0.22, 0.18) if cuts else 1.0
    values = jax.random.normal(key, extent, jnp.float32) * width * gain
    return jnp.minimum(jnp.maximum(values, -reach), reach).astype(held_as)


def setup_inputs(seed: int = 0) -> dict:
    splits = jax.random.split(jax.random.key(seed), 7)
    return {
        "b_three": noise(splits[0], (O, V, X), 0.08, 0.47851562, ((0, 32),)),
        "e_occ": jnp.clip(jax.random.uniform(splits[1], (O,), jnp.float32, -1.5, -0.3), -1.5, -0.3),
        "e_vir": jnp.clip(jax.random.uniform(splits[2], (V,), jnp.float32, 0.2, 3.0), 0.2, 3.0),
        "c_occ": noise(splits[3], (NBF, O), O ** -0.5, 0.75),
        "pair_list": draw_pair_list(jax.random.fold_in(splits[6], 71), 0),
        "pair_live": draw_pair_live(jax.random.fold_in(splits[6], 71), 0),
    }


def reference(b_three, e_occ, e_vir, c_occ, pair_list, pair_live):
    flat_pairs = pair_list.reshape(-1, 2)
    flat_live = pair_live.reshape(-1)
    gamma = jnp.zeros(b_three.shape, jnp.float32)

    def advance(index, gamma):
        first_orb = flat_pairs[index, 0].astype(jnp.int32)
        second_orb = flat_pairs[index, 1].astype(jnp.int32)

        def accumulate(gamma):
            left_slab = lax.dynamic_index_in_dim(b_three, first_orb, 0, keepdims=False)
            right_slab = lax.dynamic_index_in_dim(b_three, second_orb, 0, keepdims=False)
            integrals = lax.dot_general(left_slab, right_slab, (((1,), (1,)), ((), ())), preferred_element_type=jnp.float32)
            denominator = (e_occ[first_orb] + e_occ[second_orb]) - e_vir[:, None] - e_vir[None, :]
            amplitude = integrals / denominator
            weighted = (2.0 * amplitude - amplitude.T).astype(jnp.bfloat16)
            addition = jnp.dot(weighted, right_slab, preferred_element_type=jnp.float32)
            current = lax.dynamic_index_in_dim(gamma, first_orb, 0, keepdims=False)
            return lax.dynamic_update_index_in_dim(gamma, current + addition, first_orb, 0)

        return lax.cond(flat_live[index] > 0, accumulate, lambda kept: kept, gamma)

    gamma = lax.fori_loop(0, flat_pairs.shape[0], advance, gamma)
    moved = gamma.astype(jnp.bfloat16).reshape(gamma.shape[0], -1)
    result = lax.dot_general(moved, c_occ, (((0,), (1,)), ((), ())), preferred_element_type=jnp.float32).astype(jnp.bfloat16)
    return result.reshape(b_three.shape[1], b_three.shape[2], c_occ.shape[0])
```

```python
import functools

import jax
import jax.numpy as jnp
from jax import lax
from jax.experimental import pallas as pl
from jax.experimental.pallas import tpu as pltpu
from jax.sharding import PartitionSpec as P

CHUNKS = 4


def grid_of(peer_count):
    nx = 1
    while (2 * nx) ** 2 <= peer_count:
        nx *= 2
    return peer_count // nx, nx


def exchange_kernel(
    nz, nx, want_ref, b_ref, right_ref, up_buf, dn_buf, stage,
    up_send, up_recv, dn_send, dn_recv, keep_sem, x_send, x_recv,
):
    own_count = b_ref.shape[0]
    rows = b_ref.shape[1] // CHUNKS
    col = lax.axis_index("col")
    z, x = col // nx, col % nx

    def at(zz, xx):
        return {"col": zz * nx + xx}

    def block(c):
        return pl.ds(pl.multiple_of(c * rows, rows), rows)

    barrier = pltpu.get_barrier_semaphore()

    @pl.when(z + 1 < nz)
    def _():
        pl.semaphore_signal(barrier, inc=1, device_id=at(z + 1, x))

    @pl.when(z > 0)
    def _():
        pl.semaphore_signal(barrier, inc=1, device_id=at(z - 1, x))

    for k in range(1, nx):
        pl.semaphore_signal(barrier, inc=1, device_id=at(z, (x + k) % nx))
    greeted = (nx - 1) + (z + 1 < nz).astype(jnp.int32) + (z > 0).astype(jnp.int32)
    pl.semaphore_wait(barrier, greeted)

    def up_copy(source, hop, c):
        return pltpu.make_async_remote_copy(
            src_ref=source, dst_ref=up_buf.at[hop, :, block(c), :],
            send_sem=up_send.at[hop, c], recv_sem=up_recv.at[hop, c],
            device_id=at(z + 1, x))

    def dn_copy(source, hop, c):
        return pltpu.make_async_remote_copy(
            src_ref=source, dst_ref=dn_buf.at[hop, :, block(c), :],
            send_sem=dn_send.at[hop, c], recv_sem=dn_recv.at[hop, c],
            device_id=at(z - 1, x))

    def keep_copy(zs, c):
        return pltpu.make_async_copy(
            stage.at[0, zs, block(c), :], right_ref.at[zs * nx + x, block(c), :],
            keep_sem.at[zs, c])

    def x_copy(k, zs, c):
        return pltpu.make_async_remote_copy(
            src_ref=stage.at[k, zs, block(c), :],
            dst_ref=right_ref.at[zs * nx + x, block(c), :],
            send_sem=x_send.at[k - 1, zs, c], recv_sem=x_recv.at[k - 1, zs, c],
            device_id=at(z, (x + k) % nx))

    def hand_on(load, zs, c):
        for k in list(range(1, nx)) + [0]:
            slot = want_ref[k, zs]
            picked = load(0)
            for orb in range(1, own_count):
                picked = jnp.where(slot == orb, load(orb), picked)
            stage[k, zs, block(c), :] = picked
            if k:
                x_copy(k, zs, c).start()
            else:
                keep_copy(zs, c).start()

    def begin(c, carry):
        @pl.when(z + 1 < nz)
        def _():
            up_copy(b_ref.at[:, block(c), :], 0, c).start()

        @pl.when(z > 0)
        def _():
            dn_copy(b_ref.at[:, block(c), :], 0, c).start()

        return carry

    lax.fori_loop(0, CHUNKS, begin, 0)

    def own(c, carry):
        hand_on(lambda orb: b_ref[orb, block(c), :], z, c)
        return carry

    lax.fori_loop(0, CHUNKS, own, 0)

    for hop in range(nz - 1):
        def arrive(c, carry, hop=hop):
            @pl.when(z - hop - 1 >= 0)
            def _():
                up_copy(up_buf.at[hop, :, block(c), :], hop, c).wait_recv()
                if hop + 1 < nz - 1:
                    @pl.when(z + 1 < nz)
                    def _():
                        up_copy(up_buf.at[hop, :, block(c), :], hop + 1, c).start()

            @pl.when(z + hop + 1 < nz)
            def _():
                dn_copy(dn_buf.at[hop, :, block(c), :], hop, c).wait_recv()
                if hop + 1 < nz - 1:
                    @pl.when(z > 0)
                    def _():
                        dn_copy(dn_buf.at[hop, :, block(c), :], hop + 1, c).start()

            @pl.when(z - hop - 1 >= 0)
            def _():
                hand_on(lambda orb: up_buf[hop, orb, block(c), :], z - hop - 1, c)

            @pl.when(z + hop + 1 < nz)
            def _():
                hand_on(lambda orb: dn_buf[hop, orb, block(c), :], z + hop + 1, c)

            return carry

        lax.fori_loop(0, CHUNKS, arrive, 0)

    def finish(c, carry):
        for zs in range(nz):
            keep_copy(zs, c).wait()
            for k in range(1, nx):
                x_copy(k, zs, c).wait()
        for hop in range(nz - 1):
            @pl.when((z + 1 < nz) & (z - hop >= 0))
            def _():
                up_copy(b_ref.at[:, block(c), :], hop, c).wait_send()

            @pl.when((z > 0) & (z + hop < nz))
            def _():
                dn_copy(b_ref.at[:, block(c), :], hop, c).wait_send()
        return carry

    lax.fori_loop(0, CHUNKS, finish, 0)


def exchange(b_three, want, nz, nx):
    own_count, virt, aux = b_three.shape
    dma = pltpu.SemaphoreType.DMA
    return pl.pallas_call(
        functools.partial(exchange_kernel, nz, nx),
        out_shape=jax.ShapeDtypeStruct((nz * nx, virt, aux), b_three.dtype),
        in_specs=[
            pl.BlockSpec(memory_space=pltpu.SMEM),
            pl.BlockSpec(memory_space=pltpu.VMEM),
        ],
        out_specs=pl.BlockSpec(memory_space=pl.ANY),
        scratch_shapes=[
            pltpu.VMEM((nz - 1, own_count, virt, aux), b_three.dtype),
            pltpu.VMEM((nz - 1, own_count, virt, aux), b_three.dtype),
            pltpu.VMEM((nx, nz, virt, aux), b_three.dtype),
            dma((nz - 1, CHUNKS)), dma((nz - 1, CHUNKS)),
            dma((nz - 1, CHUNKS)), dma((nz - 1, CHUNKS)),
            dma((nz, CHUNKS)),
            dma((nx - 1, nz, CHUNKS)), dma((nx - 1, nz, CHUNKS)),
        ],
        compiler_params=pltpu.CompilerParams(
            collective_id=0, has_side_effects=True, vmem_limit_bytes=56 << 20
        ),
    )(want, b_three)


def pairs_kernel(
    slot_ref, live_ref, esum_ref, b_ref, right_ref, evc_ref, evr_ref, out_ref, gamma
):
    p = pl.program_id(0)

    @pl.when(p == 0)
    def _():
        gamma[...] = jnp.zeros_like(gamma)

    @pl.when(live_ref[p] > 0)
    def _():
        slot = slot_ref[p]
        right = right_ref[0]
        integrals = lax.dot_general(
            b_ref[slot], right, (((1,), (1,)), ((), ())), preferred_element_type=jnp.float32
        )
        amplitude = integrals / (esum_ref[p] - evc_ref[...] - evr_ref[...])
        weighted = (2.0 * amplitude - amplitude.T).astype(jnp.bfloat16)
        gamma[slot] += jnp.dot(weighted, right, preferred_element_type=jnp.float32)

    @pl.when(p == pl.num_programs(0) - 1)
    def _():
        out_ref[...] = gamma[...].astype(out_ref.dtype)


def form_pairs(b_three, right, slot, live, esum, e_vir):
    own_count, virt, aux = b_three.shape
    peers = right.shape[0]
    whole = lambda p, *_: (0, 0, 0)
    flat = lambda p, *_: (0, 0)
    return pl.pallas_call(
        pairs_kernel,
        out_shape=jax.ShapeDtypeStruct(b_three.shape, jnp.bfloat16),
        grid_spec=pltpu.PrefetchScalarGridSpec(
            num_scalar_prefetch=3,
            grid=(peers,),
            in_specs=[
                pl.BlockSpec((own_count, virt, aux), whole),
                pl.BlockSpec((1, virt, aux), lambda p, *_: (p, 0, 0)),
                pl.BlockSpec((virt, 1), flat),
                pl.BlockSpec((1, virt), flat),
            ],
            out_specs=pl.BlockSpec((own_count, virt, aux), whole),
            scratch_shapes=[pltpu.VMEM((own_count, virt, aux), jnp.float32)],
        ),
        compiler_params=pltpu.CompilerParams(vmem_limit_bytes=56 << 20),
    )(slot, live, esum, b_three, right, e_vir[:, None], e_vir[None, :])


def local(b_three, e_occ, e_vir, c_occ, pair_list, pair_live):
    own_count, virt_count, aux_count = b_three.shape
    peer_count = lax.axis_size("col")
    row_count = lax.axis_size("row")
    nz, nx = grid_of(peer_count)

    first, second = pair_list[0, :, 0], pair_list[0, :, 1]
    x = lax.axis_index("col") % nx
    slots = (second % own_count).reshape(nz, nx)
    wants = [slots]
    for k in range(1, nx):
        back = [(z * nx + (c + k) % nx, z * nx + c) for z in range(nz) for c in range(nx)]
        wants.append(lax.ppermute(slots, "col", back))
    want = lax.dynamic_index_in_dim(jnp.stack(wants), x, 2, keepdims=False)
    right = exchange(b_three, want, nz, nx)
    gamma_mo = form_pairs(
        b_three, right, first % own_count, pair_live[0], e_occ[first] + e_occ[second], e_vir
    )

    virt_local = virt_count // row_count
    aux_local = aux_count // peer_count
    total_orbs = c_occ.shape[1]
    blocks = gamma_mo.reshape(own_count, row_count, virt_local, peer_count, aux_local)
    blocks = jnp.transpose(blocks, (1, 3, 0, 2, 4)).reshape(
        row_count * peer_count, own_count, virt_local * aux_local
    )
    regrouped = lax.all_to_all(blocks, ("row", "col"), split_axis=0, concat_axis=0, tiled=True)
    moved = regrouped.reshape(total_orbs, virt_local * aux_local)
    result = lax.dot_general(
        moved, c_occ, (((0,), (1,)), ((), ())), preferred_element_type=jnp.float32
    ).astype(jnp.bfloat16)
    return result.reshape(virt_local, aux_local, c_occ.shape[0])


def solution(mesh):
    return jax.shard_map(
        local,
        mesh=mesh,
        in_specs=(
            P(("row", "col"), None, None),
            P(),
            P(),
            P(),
            P(("row", "col"), None, None),
            P(("row", "col"), None),
        ),
        out_specs=P("row", "col", None),
        check_vma=False,
    )
```

```python
import functools

import jax
import jax.numpy as jnp
from jax import lax
from jax.experimental import pallas as pl
from jax.experimental.pallas import tpu as pltpu
from jax.sharding import PartitionSpec as P

CHUNKS = 4


def grid_of(peer_count):
    nx = 1
    while (2 * nx) ** 2 <= peer_count:
        nx *= 2
    return peer_count // nx, nx


def exchange_kernel(
    nz, nx, want_ref, b_ref, right_ref, up_buf, dn_buf, stage,
    up_send, up_recv, dn_send, dn_recv, keep_sem, x_send, x_recv,
):
    own_count = b_ref.shape[0]
    rows = b_ref.shape[1] // CHUNKS
    col = lax.axis_index("col")
    z, x = col // nx, col % nx

    def at(zz, xx):
        return {"col": zz * nx + xx}

    def block(c):
        return pl.ds(pl.multiple_of(c * rows, rows), rows)

    barrier = pltpu.get_barrier_semaphore()

    @pl.when(z + 1 < nz)
    def _():
        pl.semaphore_signal(barrier, inc=1, device_id=at(z + 1, x))

    @pl.when(z > 0)
    def _():
        pl.semaphore_signal(barrier, inc=1, device_id=at(z - 1, x))

    for k in range(1, nx):
        pl.semaphore_signal(barrier, inc=1, device_id=at(z, (x + k) % nx))
    greeted = (nx - 1) + (z + 1 < nz).astype(jnp.int32) + (z > 0).astype(jnp.int32)
    pl.semaphore_wait(barrier, greeted)

    def up_copy(source, hop, c):
        return pltpu.make_async_remote_copy(
            src_ref=source, dst_ref=up_buf.at[hop, :, block(c), :],
            send_sem=up_send.at[hop, c], recv_sem=up_recv.at[hop, c],
            device_id=at(z + 1, x))

    def dn_copy(source, hop, c):
        return pltpu.make_async_remote_copy(
            src_ref=source, dst_ref=dn_buf.at[hop, :, block(c), :],
            send_sem=dn_send.at[hop, c], recv_sem=dn_recv.at[hop, c],
            device_id=at(z - 1, x))

    def keep_copy(zs, c):
        return pltpu.make_async_copy(
            stage.at[0, zs, block(c), :], right_ref.at[zs * nx + x, block(c), :],
            keep_sem.at[zs, c])

    def x_copy(k, zs, c):
        return pltpu.make_async_remote_copy(
            src_ref=stage.at[k, zs, block(c), :],
            dst_ref=right_ref.at[zs * nx + x, block(c), :],
            send_sem=x_send.at[k - 1, zs, c], recv_sem=x_recv.at[k - 1, zs, c],
            device_id=at(z, (x + k) % nx))

    def hand_on(load, zs, c):
        for k in list(range(1, nx)) + [0]:
            slot = want_ref[k, zs * nx + x, 1] % own_count
            picked = load(0)
            for orb in range(1, own_count):
                picked = jnp.where(slot == orb, load(orb), picked)
            stage[k, zs, block(c), :] = picked
            if k:
                x_copy(k, zs, c).start()
            else:
                keep_copy(zs, c).start()

    def begin(c, carry):
        @pl.when(z + 1 < nz)
        def _():
            up_copy(b_ref.at[:, block(c), :], 0, c).start()

        @pl.when(z > 0)
        def _():
            dn_copy(b_ref.at[:, block(c), :], 0, c).start()

        return carry

    lax.fori_loop(0, CHUNKS, begin, 0)

    def own(c, carry):
        hand_on(lambda orb: b_ref[orb, block(c), :], z, c)
        return carry

    lax.fori_loop(0, CHUNKS, own, 0)

    for hop in range(nz - 1):
        def arrive(c, carry, hop=hop):
            @pl.when(z - hop - 1 >= 0)
            def _():
                up_copy(up_buf.at[hop, :, block(c), :], hop, c).wait_recv()
                if hop + 1 < nz - 1:
                    @pl.when(z + 1 < nz)
                    def _():
                        up_copy(up_buf.at[hop, :, block(c), :], hop + 1, c).start()

            @pl.when(z + hop + 1 < nz)
            def _():
                dn_copy(dn_buf.at[hop, :, block(c), :], hop, c).wait_recv()
                if hop + 1 < nz - 1:
                    @pl.when(z > 0)
                    def _():
                        dn_copy(dn_buf.at[hop, :, block(c), :], hop + 1, c).start()

            @pl.when(z - hop - 1 >= 0)
            def _():
                hand_on(lambda orb: up_buf[hop, orb, block(c), :], z - hop - 1, c)

            @pl.when(z + hop + 1 < nz)
            def _():
                hand_on(lambda orb: dn_buf[hop, orb, block(c), :], z + hop + 1, c)

            return carry

        lax.fori_loop(0, CHUNKS, arrive, 0)

    def finish(c, carry):
        for zs in range(nz):
            keep_copy(zs, c).wait()
            for k in range(1, nx):
                x_copy(k, zs, c).wait()
        for hop in range(nz - 1):
            @pl.when((z + 1 < nz) & (z - hop >= 0))
            def _():
                up_copy(b_ref.at[:, block(c), :], hop, c).wait_send()

            @pl.when((z > 0) & (z + hop < nz))
            def _():
                dn_copy(b_ref.at[:, block(c), :], hop, c).wait_send()
        return carry

    lax.fori_loop(0, CHUNKS, finish, 0)


def exchange(b_three, want, nz, nx):
    own_count, virt, aux = b_three.shape
    dma = pltpu.SemaphoreType.DMA
    return pl.pallas_call(
        functools.partial(exchange_kernel, nz, nx),
        out_shape=jax.ShapeDtypeStruct((nz * nx, virt, aux), b_three.dtype),
        in_specs=[
            pl.BlockSpec(memory_space=pltpu.SMEM),
            pl.BlockSpec(memory_space=pltpu.VMEM),
        ],
        out_specs=pl.BlockSpec(memory_space=pl.ANY),
        scratch_shapes=[
            pltpu.VMEM((nz - 1, own_count, virt, aux), b_three.dtype),
            pltpu.VMEM((nz - 1, own_count, virt, aux), b_three.dtype),
            pltpu.VMEM((nx, nz, virt, aux), b_three.dtype),
            dma((nz - 1, CHUNKS)), dma((nz - 1, CHUNKS)),
            dma((nz - 1, CHUNKS)), dma((nz - 1, CHUNKS)),
            dma((nz, CHUNKS)),
            dma((nx - 1, nz, CHUNKS)), dma((nx - 1, nz, CHUNKS)),
        ],
        compiler_params=pltpu.CompilerParams(
            collective_id=0, has_side_effects=True, vmem_limit_bytes=56 << 20
        ),
    )(want, b_three)


def pieces_of(start, width):
    found = []
    while width:
        tile, lane = start // 128, start % 128
        length = min(width, 128 - lane)
        found.append((tile, lane, length))
        start, width = start + length, width - length
    return found


def pairs_kernel(
    row_count, peers, pair_ref, live_ref, occ_ref, b_ref, right_ref, ev_ref, out_ref,
    gamma, down, flat,
):
    p = pl.program_id(0)
    own_count, virt, aux = b_ref.shape
    tiles = aux // 128
    virt_local, aux_local = virt // row_count, aux // peers
    group = 1
    while group * aux_local % 128:
        group *= 2

    @pl.when(p == 0)
    def _():
        gamma[...] = jnp.zeros_like(gamma)
        down[...] = jnp.broadcast_to(ev_ref[...], (virt, virt)).T

    @pl.when(live_ref[p] > 0)
    def _():
        first, second = pair_ref[p, 0], pair_ref[p, 1]
        slot = first % own_count
        right = right_ref[0]
        integrals = lax.dot_general(
            b_ref[slot], right, (((1,), (1,)), ((), ())), preferred_element_type=jnp.float32
        )
        amplitude = integrals / (occ_ref[first] + occ_ref[second] - down[...] - ev_ref[...])
        weighted = (2.0 * amplitude - amplitude.T).astype(jnp.bfloat16)
        addition = jnp.dot(weighted, right, preferred_element_type=jnp.float32)
        for t in range(tiles):
            gamma[slot, t] += addition[:, 128 * t:128 * (t + 1)]

    @pl.when(p == peers - 1)
    def _():
        count = virt_local // group
        per = group * aux_local // 128

        def emit(step, carry):
            orb, r = step // row_count, step % row_count
            for c in range(peers):
                for t in range(per):
                    parts = []
                    for j, lane, length in [
                        (f // aux_local, f % aux_local, min(aux_local - f % aux_local, 128 * (t + 1) - f))
                        for f in sorted({128 * t} | {j * aux_local for j in range(group) if 128 * t < j * aux_local < 128 * (t + 1)})
                    ]:
                        for tile, at, size in pieces_of(c * aux_local + lane, length):
                            rows = gamma[orb, tile, pl.ds(r * virt_local + j, count, stride=group), :]
                            parts.append(rows if size == 128 else rows[:, at:at + size])
                    joined = parts[0] if len(parts) == 1 else jnp.concatenate(parts, axis=1)
                    flat[c, pl.ds(t, count, stride=per), :] = joined
                out_ref[r * peers + c, orb] = flat[c].astype(out_ref.dtype)
            return carry

        lax.fori_loop(0, own_count * row_count, emit, 0)


def form_pairs(b_three, right, pairs, live, e_occ, e_vir, row_count):
    own_count, virt, aux = b_three.shape
    peers = right.shape[0]
    whole = lambda p, *_: (0, 0, 0)
    lines = virt * aux // (row_count * peers * 128)
    shape = (row_count * peers, own_count, lines, 128)
    return pl.pallas_call(
        functools.partial(pairs_kernel, row_count, peers),
        out_shape=jax.ShapeDtypeStruct(shape, jnp.bfloat16),
        grid_spec=pltpu.PrefetchScalarGridSpec(
            num_scalar_prefetch=3,
            grid=(peers,),
            in_specs=[
                pl.BlockSpec((own_count, virt, aux), whole),
                pl.BlockSpec((1, virt, aux), lambda p, *_: (p, 0, 0)),
                pl.BlockSpec((1, virt), lambda p, *_: (0, 0)),
            ],
            out_specs=pl.BlockSpec(shape, lambda p, *_: (0, 0, 0, 0)),
            scratch_shapes=[
                pltpu.VMEM((own_count, aux // 128, virt, 128), jnp.float32),
                pltpu.VMEM((virt, virt), jnp.float32),
                pltpu.VMEM((peers, lines, 128), jnp.float32),
            ],
        ),
        compiler_params=pltpu.CompilerParams(vmem_limit_bytes=56 << 20),
    )(pairs, live, e_occ, b_three, right, e_vir[None, :])


def spread_kernel(row_count, peers, src_ref, dst_ref, keep_sem, send_sem, recv_sem):
    n = row_count * peers
    me = lax.axis_index("row") * peers + lax.axis_index("col")

    def partner(k):
        d = (me + k) % n
        return d, {"row": d // peers, "col": d % peers}

    barrier = pltpu.get_barrier_semaphore()

    def greet(k, carry):
        pl.semaphore_signal(barrier, inc=1, device_id=partner(k)[1])
        return carry

    lax.fori_loop(1, n, greet, 0)
    pl.semaphore_wait(barrier, n - 1)
    keep = pltpu.make_async_copy(src_ref.at[me], dst_ref.at[me], keep_sem)
    keep.start()

    def copy(k):
        d, where = partner(k)
        return pltpu.make_async_remote_copy(
            src_ref=src_ref.at[d], dst_ref=dst_ref.at[me],
            send_sem=send_sem.at[k], recv_sem=recv_sem.at[k], device_id=where)

    def begin(k, carry):
        copy(k).start()
        return carry

    def finish(k, carry):
        copy(k).wait()
        return carry

    lax.fori_loop(1, n, begin, 0)
    lax.fori_loop(1, n, finish, 0)
    keep.wait()


def spread(blocks, row_count, peers):
    n = row_count * peers
    return pl.pallas_call(
        functools.partial(spread_kernel, row_count, peers),
        out_shape=jax.ShapeDtypeStruct(blocks.shape, blocks.dtype),
        in_specs=[pl.BlockSpec(memory_space=pl.ANY)],
        out_specs=pl.BlockSpec(memory_space=pl.ANY),
        scratch_shapes=[
            pltpu.SemaphoreType.DMA, pltpu.SemaphoreType.DMA((n,)), pltpu.SemaphoreType.DMA((n,)),
        ],
        compiler_params=pltpu.CompilerParams(collective_id=1, has_side_effects=True),
    )(blocks)


def local(b_three, e_occ, e_vir, c_occ, pair_list, pair_live):
    own_count, virt_count, aux_count = b_three.shape
    peer_count = lax.axis_size("col")
    row_count = lax.axis_size("row")
    nz, nx = grid_of(peer_count)

    tables = [pair_list]
    for k in range(1, nx):
        back = [(z * nx + (c + k) % nx, z * nx + c) for z in range(nz) for c in range(nx)]
        tables.append(lax.ppermute(pair_list, "col", back))
    right = exchange(b_three, jnp.concatenate(tables), nz, nx)
    blocks = form_pairs(
        b_three, right, pair_list[0], pair_live[0], e_occ, e_vir, row_count
    )

    regrouped = spread(blocks, row_count, peer_count)
    virt_local = virt_count // row_count
    aux_local = aux_count // peer_count
    moved = regrouped.reshape(c_occ.shape[1], virt_local * aux_local)
    result = lax.dot_general(
        moved, c_occ, (((0,), (1,)), ((), ())), preferred_element_type=jnp.float32
    ).astype(jnp.bfloat16)
    return result.reshape(virt_local, aux_local, c_occ.shape[0])


def solution(mesh):
    return jax.shard_map(
        local,
        mesh=mesh,
        in_specs=(
            P(("row", "col"), None, None),
            P(),
            P(),
            P(),
            P(("row", "col"), None, None),
            P(("row", "col"), None),
        ),
        out_specs=P("row", "col", None),
        check_vma=False,
    )
```

```python
import functools

import jax
import jax.numpy as jnp
from jax import lax
from jax.experimental import pallas as pl
from jax.experimental.pallas import tpu as pltpu
from jax.sharding import PartitionSpec as P

CHUNKS = 8


def grid_of(peer_count):
    nx = 1
    while (2 * nx) ** 2 <= peer_count:
        nx *= 2
    return peer_count // nx, nx


def exchange_kernel(
    nz, nx, want_ref, b_ref, right_ref, up_buf, dn_buf, stage,
    up_send, up_recv, dn_send, dn_recv, keep_sem, x_send, x_recv,
):
    own_count = b_ref.shape[0]
    rows = b_ref.shape[1] // CHUNKS
    col = lax.axis_index("col")
    z, x = col // nx, col % nx

    def at(zz, xx):
        return {"col": zz * nx + xx}

    def block(c):
        return pl.ds(pl.multiple_of(c * rows, rows), rows)

    barrier = pltpu.get_barrier_semaphore()

    @pl.when(z + 1 < nz)
    def _():
        pl.semaphore_signal(barrier, inc=1, device_id=at(z + 1, x))

    @pl.when(z > 0)
    def _():
        pl.semaphore_signal(barrier, inc=1, device_id=at(z - 1, x))

    for k in range(1, nx):
        pl.semaphore_signal(barrier, inc=1, device_id=at(z, (x + k) % nx))
    greeted = (nx - 1) + (z + 1 < nz).astype(jnp.int32) + (z > 0).astype(jnp.int32)
    pl.semaphore_wait(barrier, greeted)

    def up_copy(source, hop, c):
        return pltpu.make_async_remote_copy(
            src_ref=source, dst_ref=up_buf.at[hop, :, block(c), :],
            send_sem=up_send.at[hop, c], recv_sem=up_recv.at[hop, c],
            device_id=at(z + 1, x))

    def dn_copy(source, hop, c):
        return pltpu.make_async_remote_copy(
            src_ref=source, dst_ref=dn_buf.at[hop, :, block(c), :],
            send_sem=dn_send.at[hop, c], recv_sem=dn_recv.at[hop, c],
            device_id=at(z - 1, x))

    def keep_copy(zs, c):
        return pltpu.make_async_copy(
            stage.at[0, zs, block(c), :], right_ref.at[zs * nx + x, block(c), :],
            keep_sem.at[zs, c])

    def x_copy(k, zs, c):
        return pltpu.make_async_remote_copy(
            src_ref=stage.at[k, zs, block(c), :],
            dst_ref=right_ref.at[zs * nx + x, block(c), :],
            send_sem=x_send.at[k - 1, zs, c], recv_sem=x_recv.at[k - 1, zs, c],
            device_id=at(z, (x + k) % nx))

    def hand_on(load, zs, c):
        for k in list(range(1, nx)) + [0]:
            slot = want_ref[k, zs * nx + x, 1] % own_count
            picked = load(0)
            for orb in range(1, own_count):
                picked = jnp.where(slot == orb, load(orb), picked)
            stage[k, zs, block(c), :] = picked
            if k:
                x_copy(k, zs, c).start()
            else:
                keep_copy(zs, c).start()

    def begin(c, carry):
        @pl.when(z + 1 < nz)
        def _():
            up_copy(b_ref.at[:, block(c), :], 0, c).start()

        @pl.when(z > 0)
        def _():
            dn_copy(b_ref.at[:, block(c), :], 0, c).start()

        return carry

    lax.fori_loop(0, CHUNKS, begin, 0)

    def own(c, carry):
        hand_on(lambda orb: b_ref[orb, block(c), :], z, c)
        return carry

    lax.fori_loop(0, CHUNKS, own, 0)

    for hop in range(nz - 1):
        def arrive(c, carry, hop=hop):
            @pl.when(z - hop - 1 >= 0)
            def _():
                up_copy(up_buf.at[hop, :, block(c), :], hop, c).wait_recv()
                if hop + 1 < nz - 1:
                    @pl.when(z + 1 < nz)
                    def _():
                        up_copy(up_buf.at[hop, :, block(c), :], hop + 1, c).start()

            @pl.when(z + hop + 1 < nz)
            def _():
                dn_copy(dn_buf.at[hop, :, block(c), :], hop, c).wait_recv()
                if hop + 1 < nz - 1:
                    @pl.when(z > 0)
                    def _():
                        dn_copy(dn_buf.at[hop, :, block(c), :], hop + 1, c).start()

            @pl.when(z - hop - 1 >= 0)
            def _():
                hand_on(lambda orb: up_buf[hop, orb, block(c), :], z - hop - 1, c)

            @pl.when(z + hop + 1 < nz)
            def _():
                hand_on(lambda orb: dn_buf[hop, orb, block(c), :], z + hop + 1, c)

            return carry

        lax.fori_loop(0, CHUNKS, arrive, 0)

    def finish(c, carry):
        for zs in range(nz):
            keep_copy(zs, c).wait()
            for k in range(1, nx):
                x_copy(k, zs, c).wait()
        for hop in range(nz - 1):
            @pl.when((z + 1 < nz) & (z - hop >= 0))
            def _():
                up_copy(b_ref.at[:, block(c), :], hop, c).wait_send()

            @pl.when((z > 0) & (z + hop < nz))
            def _():
                dn_copy(b_ref.at[:, block(c), :], hop, c).wait_send()
        return carry

    lax.fori_loop(0, CHUNKS, finish, 0)


def exchange(b_three, want, nz, nx):
    own_count, virt, aux = b_three.shape
    dma = pltpu.SemaphoreType.DMA
    return pl.pallas_call(
        functools.partial(exchange_kernel, nz, nx),
        out_shape=jax.ShapeDtypeStruct((nz * nx, virt, aux), b_three.dtype),
        in_specs=[
            pl.BlockSpec(memory_space=pltpu.SMEM),
            pl.BlockSpec(memory_space=pltpu.VMEM),
        ],
        out_specs=pl.BlockSpec(memory_space=pl.ANY),
        scratch_shapes=[
            pltpu.VMEM((nz - 1, own_count, virt, aux), b_three.dtype),
            pltpu.VMEM((nz - 1, own_count, virt, aux), b_three.dtype),
            pltpu.VMEM((nx, nz, virt, aux), b_three.dtype),
            dma((nz - 1, CHUNKS)), dma((nz - 1, CHUNKS)),
            dma((nz - 1, CHUNKS)), dma((nz - 1, CHUNKS)),
            dma((nz, CHUNKS)),
            dma((nx - 1, nz, CHUNKS)), dma((nx - 1, nz, CHUNKS)),
        ],
        compiler_params=pltpu.CompilerParams(
            collective_id=0, has_side_effects=True, vmem_limit_bytes=56 << 20
        ),
    )(want, b_three)


def pieces_of(start, width):
    found = []
    while width:
        tile, lane = start // 128, start % 128
        length = min(width, 128 - lane)
        found.append((tile, lane, length))
        start, width = start + length, width - length
    return found


def pairs_kernel(
    row_count, peers, pair_ref, live_ref, occ_ref, b_ref, right_ref, ev_ref, out_ref,
    gamma, down, flat,
):
    p = pl.program_id(0)
    own_count, virt, aux = b_ref.shape
    tiles = aux // 128
    virt_local, aux_local = virt // row_count, aux // peers
    group = 1
    while group * aux_local % 128:
        group *= 2

    @pl.when(p == 0)
    def _():
        gamma[...] = jnp.zeros_like(gamma)
        down[...] = jnp.broadcast_to(ev_ref[...][None, :], (virt, virt)).T

    @pl.when(live_ref[0, p] > 0)
    def _():
        first, second = pair_ref[0, p, 0], pair_ref[0, p, 1]
        slot = first % own_count
        right = right_ref[0]
        integrals = lax.dot_general(
            b_ref[slot], right, (((1,), (1,)), ((), ())), preferred_element_type=jnp.float32
        )
        amplitude = integrals / (occ_ref[first] + occ_ref[second] - down[...] - ev_ref[...][None, :])
        weighted = (2.0 * amplitude - amplitude.T).astype(jnp.bfloat16)
        addition = jnp.dot(weighted, right, preferred_element_type=jnp.float32)
        for t in range(tiles):
            gamma[slot, t] += addition[:, 128 * t:128 * (t + 1)]

    @pl.when(p == peers - 1)
    def _():
        count = virt_local // group
        per = group * aux_local // 128

        def emit(step, carry):
            orb, r = step // row_count, step % row_count
            for c in range(peers):
                for t in range(per):
                    parts = []
                    for j, lane, length in [
                        (f // aux_local, f % aux_local, min(aux_local - f % aux_local, 128 * (t + 1) - f))
                        for f in sorted({128 * t} | {j * aux_local for j in range(group) if 128 * t < j * aux_local < 128 * (t + 1)})
                    ]:
                        for tile, at, size in pieces_of(c * aux_local + lane, length):
                            rows = gamma[orb, tile, pl.ds(r * virt_local + j, count, stride=group), :]
                            parts.append(rows if size == 128 else rows[:, at:at + size])
                    joined = parts[0] if len(parts) == 1 else jnp.concatenate(parts, axis=1)
                    flat[c, pl.ds(t, count, stride=per), :] = joined
                out_ref[r * peers + c, orb] = flat[c].astype(out_ref.dtype)
            return carry

        lax.fori_loop(0, own_count * row_count, emit, 0)


def form_pairs(b_three, right, pairs, live, e_occ, e_vir, row_count):
    own_count, virt, aux = b_three.shape
    peers = right.shape[0]
    whole = lambda p, *_: (0, 0, 0)
    lines = virt * aux // (row_count * peers * 128)
    shape = (row_count * peers, own_count, lines, 128)
    return pl.pallas_call(
        functools.partial(pairs_kernel, row_count, peers),
        out_shape=jax.ShapeDtypeStruct(shape, jnp.bfloat16),
        grid_spec=pltpu.PrefetchScalarGridSpec(
            num_scalar_prefetch=3,
            grid=(peers,),
            in_specs=[
                pl.BlockSpec((own_count, virt, aux), whole),
                pl.BlockSpec((1, virt, aux), lambda p, *_: (p, 0, 0)),
                pl.BlockSpec((virt,), lambda p, *_: (0,)),
            ],
            out_specs=pl.BlockSpec(shape, lambda p, *_: (0, 0, 0, 0)),
            scratch_shapes=[
                pltpu.VMEM((own_count, aux // 128, virt, 128), jnp.float32),
                pltpu.VMEM((virt, virt), jnp.float32),
                pltpu.VMEM((peers, lines, 128), jnp.float32),
            ],
        ),
        compiler_params=pltpu.CompilerParams(vmem_limit_bytes=56 << 20),
    )(pairs, live, e_occ, b_three, right, e_vir)


def spread_kernel(row_count, peers, src_ref, dst_ref, keep_sem, send_sem, recv_sem):
    n = row_count * peers
    me = lax.axis_index("row") * peers + lax.axis_index("col")

    def partner(k):
        d = (me + k) % n
        return d, {"row": d // peers, "col": d % peers}

    barrier = pltpu.get_barrier_semaphore()

    def greet(k, carry):
        pl.semaphore_signal(barrier, inc=1, device_id=partner(k)[1])
        return carry

    lax.fori_loop(1, n, greet, 0)
    pl.semaphore_wait(barrier, n - 1)
    keep = pltpu.make_async_copy(src_ref.at[me], dst_ref.at[me], keep_sem)
    keep.start()

    def copy(k):
        d, where = partner(k)
        return pltpu.make_async_remote_copy(
            src_ref=src_ref.at[d], dst_ref=dst_ref.at[me],
            send_sem=send_sem.at[k], recv_sem=recv_sem.at[k], device_id=where)

    def begin(k, carry):
        copy(k).start()
        return carry

    def finish(k, carry):
        copy(k).wait()
        return carry

    lax.fori_loop(1, n, begin, 0)
    lax.fori_loop(1, n, finish, 0)
    keep.wait()


def spread(blocks, row_count, peers):
    n = row_count * peers
    return pl.pallas_call(
        functools.partial(spread_kernel, row_count, peers),
        out_shape=jax.ShapeDtypeStruct(blocks.shape, blocks.dtype),
        in_specs=[pl.BlockSpec(memory_space=pl.ANY)],
        out_specs=pl.BlockSpec(memory_space=pl.ANY),
        scratch_shapes=[
            pltpu.SemaphoreType.DMA, pltpu.SemaphoreType.DMA((n,)), pltpu.SemaphoreType.DMA((n,)),
        ],
        compiler_params=pltpu.CompilerParams(collective_id=1, has_side_effects=True),
    )(blocks)


def local(b_three, e_occ, e_vir, c_occ, pair_list, pair_live):
    own_count, virt_count, aux_count = b_three.shape
    peer_count = lax.axis_size("col")
    row_count = lax.axis_size("row")
    nz, nx = grid_of(peer_count)

    tables = [pair_list]
    for k in range(1, nx):
        back = [(z * nx + (c + k) % nx, z * nx + c) for z in range(nz) for c in range(nx)]
        tables.append(lax.ppermute(pair_list, "col", back))
    right = exchange(b_three, jnp.concatenate(tables), nz, nx)
    blocks = form_pairs(
        b_three, right, pair_list, pair_live, e_occ, e_vir, row_count
    )

    regrouped = spread(blocks, row_count, peer_count)
    virt_local = virt_count // row_count
    aux_local = aux_count // peer_count
    moved = regrouped.reshape(c_occ.shape[1], virt_local * aux_local)
    result = lax.dot_general(
        moved, c_occ, (((0,), (1,)), ((), ())), preferred_element_type=jnp.float32
    ).astype(jnp.bfloat16)
    return result.reshape(virt_local, aux_local, c_occ.shape[0])


def solution(mesh):
    return jax.shard_map(
        local,
        mesh=mesh,
        in_specs=(
            P(("row", "col"), None, None),
            P(),
            P(),
            P(),
            P(("row", "col"), None, None),
            P(("row", "col"), None),
        ),
        out_specs=P("row", "col", None),
        check_vma=False,
    )
```
